512 devices in a mesh: dp: 64 (over z_hi, y, core), tensor: 8 (over x, z_lo).
Axes of the slice: x: 4, y: 8, z: 8 (z_hi: 4, z_lo: 2; z = z_hi * 2 + z_lo), core: 2. Of those that a mesh axis runs over, the one named last changes fastest.
Arguments:
- teacher: bfloat16 [16384, 3072], P('dp', 'tensor'), may hold values from -6 to 6
- projector: bfloat16 [3072, 2048], P('tensor', 'dp'), may hold values from -0.109375 to 0.109375
- residual: bfloat16 [16384, 2048], P(('dp', 'tensor')), may hold values from -6 to 6
- gate_pre: bfloat16 [16384, 8192], P('dp', 'tensor'), may hold values from -6 to 6
- up_pre: bfloat16 [16384, 8192], P('dp', 'tensor'), may hold values from -6 to 6
- down_weight: bfloat16 [8192, 2048], P('tensor', 'dp'), may hold values from -0.0625 to 0.0625
Outputs:
- projector_grad: float32 [3072, 2048], P('tensor', 'dp')
- grad_residual: bfloat16 [16384, 2048], P(('dp', 'tensor'))
- grad_gate: bfloat16 [16384, 8192], P('dp', 'tensor')
- grad_up: bfloat16 [16384, 8192], P('dp', 'tensor')
The draws below stay inside these ranges and needn't reach their ends.
All inputs are finite; a program needn't handle non-finite values.
Results may differ from the reference program's by a relative error of at most 0.015.
Values may be sent and summed in bfloat16 or wider, within the bound.
A program may use at most 64 MiB of HBM per device.

```python
import math
import jax
import jax.numpy as jnp

SC = 2048
TC = 3072
FF = 8192
TOKENS = 16384
N_TENSOR = 8


def shard_levels(own_key, dims, pieces, smallest, top_value):
    level = 1.0
    for dim, blocks in pieces:
        draws = jax.random.uniform(jax.random.fold_in(jax.random.fold_in(own_key, 6), dim), (blocks,), jnp.float32, smallest / len(pieces), top_value / len(pieces))
        level = level * jnp.repeat(jnp.exp(draws), dims[dim] // blocks).reshape((-1,) + (1,) * (len(dims) - 1 - dim))
    return level


def scatter_about(key, shape, width, limit, cuts=(), dtype=jnp.bfloat16):
    loudness = shard_levels(key, shape, cuts, -0.22, 0.18) if cuts else 1.0
    array = jax.random.normal(key, shape, jnp.float32) * width * loudness
    return jnp.minimum(jnp.maximum(array, -limit), limit).astype(dtype)


def setup_inputs(seed: int = 0) -> dict:
    streams_of = jax.random.split(jax.random.key(seed), 7)
    return {
        "teacher": scatter_about(streams_of[0], (TOKENS, TC), 1.0, 6.0, ((0, 64), (1, 8))),
        "projector": scatter_about(streams_of[1], (TC, SC), TC ** -0.5, 0.109375, ((0, 8), (1, 64))),
        "residual": scatter_about(streams_of[2], (TOKENS, SC), 1.0, 6.0, ((0, 512),)),
        "gate_pre": scatter_about(streams_of[3], (TOKENS, FF), 1.0, 6.0, ((0, 64), (1, 8))),
        "up_pre": scatter_about(streams_of[4], (TOKENS, FF), 1.0, 6.0, ((0, 64), (1, 8))),
        "down_weight": scatter_about(streams_of[5], (FF, SC), FF ** -0.5, 0.0625, ((0, 8), (1, 64))),
    }


def reference(teacher, projector, residual, gate_pre, up_pre, down_weight):
    gate = gate_pre.astype(jnp.float32)
    upper = up_pre.astype(jnp.float32)
    sig = jax.nn.sigmoid(gate)
    hidden = (gate * sig * upper).astype(jnp.bfloat16)
    ff_block = FF // N_TENSOR
    tc_block = TC // N_TENSOR
    total = residual.astype(jnp.float32)
    for block in range(N_TENSOR):
        mlp_term = jnp.dot(hidden[:, block * ff_block:(block + 1) * ff_block], down_weight[block * ff_block:(block + 1) * ff_block], preferred_element_type=jnp.float32)
        proj_term = jnp.dot(teacher[:, block * tc_block:(block + 1) * tc_block], projector[block * tc_block:(block + 1) * tc_block], preferred_element_type=jnp.float32)
        total = total + (mlp_term - proj_term).astype(jnp.bfloat16).astype(jnp.float32)
    grad_residual = total.astype(jnp.bfloat16)
    hidden_grad = jnp.dot(grad_residual, down_weight.T, preferred_element_type=jnp.float32)
    grad_up = (hidden_grad * gate * sig).astype(jnp.bfloat16)
    grad_gate = (hidden_grad * upper * sig * (1.0 + gate * (1.0 - sig))).astype(jnp.bfloat16)
    projector_grad = jnp.dot(teacher.T, grad_residual, preferred_element_type=jnp.float32) / math.sqrt(TOKENS)
    return (projector_grad, grad_residual, grad_gate, grad_up)
```

```python
import math

import jax
import jax.numpy as jnp
from jax import lax
from jax.experimental import pallas as pl
from jax.experimental.pallas import tpu as pltpu
from jax.sharding import PartitionSpec as P

NY, NZ, NT = 8, 4, 8
MESH = pl.DeviceIdType.MESH
F32, BF16 = jnp.float32, jnp.bfloat16
GRAY = (0, 1, 3, 2)


def kernel(
    w_in, p_in, teacher, residual, gate, up,
    pg_out, gr_out, gg_out, gu_out,
    wall, hid, parts, rbuf, rows, hgrad, lgf, lgb, lgr, ysend, yland, zsend, zland,
    bz_s, bz_r, wz_s, wz_r, wy_s, wy_r, ws_s, ws_r, ex_s, ex_r, ag_s, ag_r,
    ls_s, ls_r, ry_s, ry_r,
):
    dp = lax.axis_index("dp")
    me = lax.axis_index("tensor")
    c = lax.rem(dp, 2)
    y = lax.rem(lax.div(dp, 2), NY)
    zh = lax.div(dp, 2 * NY)

    def dev(cc, yy, zz, tt):
        return ((zz * NY + yy) * 2 + cc, tt)

    def ymod(s):
        return lax.rem(y + s + NY, NY)

    def zmod(s):
        return lax.rem(zh + s + NZ, NZ)

    sib = dev(1 - c, y, zh, me)
    up_y = dev(c, ymod(1), zh, me)
    dn_y = dev(c, ymod(-1), zh, me)

    def zdev(q):
        return dev(c, y, zmod(q), me)

    def tdev(d):
        return (dp, lax.rem(me + d, NT))

    def rc(src, dst, ssem, rsem, to):
        return pltpu.make_async_remote_copy(
            src_ref=src, dst_ref=dst, send_sem=ssem, recv_sem=rsem,
            device_id=to, device_id_type=MESH,
        )

    def loc(yy, zz, cc):
        return wall.at[lax.div(yy, 2), zz, lax.rem(yy, 2), cc]

    k0 = lax.div(y, 2)
    par = lax.rem(y, 2)
    wall[k0, zh, par, c, :, :1024] = w_in[...]
    wall[k0, zh, par, c, :, 1024:] = p_in[...]

    barrier = pltpu.get_barrier_semaphore()
    peers = [sib, up_y, dn_y] + [zdev(q) for q in (1, 2, 3)] + [tdev(d) for d in range(1, NT)]
    for to in peers:
        pl.semaphore_signal(barrier, inc=1, device_id=to, device_id_type=MESH)
    pl.semaphore_wait(barrier, len(peers))

    def wz(q):
        u = loc(y, zh, c)
        return rc(u, u, wz_s.at[q - 1], wz_r.at[q - 1], zdev(q))

    def wz_in(q):
        u = loc(y, zmod(-q), c)
        return rc(u, u, wz_s.at[q - 1], wz_r.at[q - 1], zdev(q))

    def wy(d, s, j):
        sign = 1 - 2 * d
        u = loc(ymod(-sign * (s - 1)), zmod(-j), c)
        return rc(u, u, wy_s.at[d, s - 1, j], wy_r.at[d, s - 1, j], (up_y, dn_y)[d])

    def wy_in(d, s, j):
        sign = 1 - 2 * d
        u = loc(ymod(-sign * s), zmod(-j), c)
        return rc(u, u, wy_s.at[d, s - 1, j], wy_r.at[d, s - 1, j], (up_y, dn_y)[d])

    def ws(d, s, j, cc):
        sign = 1 - 2 * d
        u = loc(ymod(-sign * s), zmod(-j), cc)
        return rc(u, u, ws_s.at[d, s, j], ws_r.at[d, s, j], sib)

    def share(d, s, j):
        ws(d, s, j, c).start()

    for q in (1, 3, 2):
        wz(q).start()
    for d in (0, 1):
        wy(d, 1, 0).start()
    share(0, 0, 0)

    @pl.loop(0, 8)
    def _(r):
        at = pl.ds(pl.multiple_of(r * 32, 32), 32)
        g = gate[at, :].astype(F32)
        u = up[at, :].astype(F32)
        hid[at, :1024] = (g * jax.nn.sigmoid(g) * u).astype(BF16)
        hid[at, 1024:] = -teacher[at, :]

    for q in (1, 3, 2):
        wz_in(q).wait_recv()
        for d in (0, 1):
            wy(d, 1, q).start()
        share(0, 0, q)

    def y_unit(s, n):
        j = GRAY[n]
        for d in (0, 1):
            if s == 4 and (n >= 2) != (d == 1):
                continue
            wy_in(d, s, j).wait_recv()
            if s < 3 or (s == 3 and (n >= 2) == (d == 1)):
                wy(d, s + 1, j).start()
            share(d, s, j)

    def sib_wait(s):
        for n in range(4):
            j = GRAY[n]
            if s == 0:
                ws(0, 0, j, 1 - c).wait_recv()
                continue
            for d in (0, 1):
                if s == 4 and (n >= 2) != (d == 1):
                    continue
                ws(d, s, j, 1 - c).wait_recv()

    turn = 2 * par - 1
    pair = [k0, lax.rem(k0 + turn + 4, 4), lax.rem(k0 - turn + 4, 4), lax.rem(k0 + 2, 4)]

    def span(i, z):
        return pl.ds(pl.multiple_of(z * 512 + pair[i] * 128, 128), 128)

    def ex(i, d):
        give = pl.ds(pl.multiple_of(lax.rem(me + d, NT) * 32, 32), 32)
        return rc(parts.at[i, give, :], rbuf.at[i, d - 1], ex_s.at[i, d - 1], ex_r.at[i, d - 1], tdev(d))

    mine = pl.ds(pl.multiple_of(me * 32, 32), 32)

    def ag(i, d):
        return rc(rows.at[i, mine, :], rows.at[i, mine, :], ag_s.at[i, d - 1], ag_r.at[i, d - 1], tdev(d))

    def ag_in(i, d):
        at = pl.ds(pl.multiple_of(lax.rem(me - d + NT, NT) * 32, 32), 32)
        return rc(rows.at[i, at, :], rows.at[i, at, :], ag_s.at[i, d - 1], ag_r.at[i, d - 1], tdev(d))

    def stage_a(i):
        w = wall[pair[i]].reshape(512, 1408)
        out = lax.dot_general(hid[...], w, (((1,), (1,)), ((), ())), preferred_element_type=F32)
        parts[i] = out.astype(BF16)
        for d in range(1, NT):
            ex(i, d).start()

    def stage_b(i):
        acc = parts[i, mine, :].astype(F32)
        for d in range(1, NT):
            ex(i, d).wait_recv()
            acc = acc + rbuf[i, d - 1].astype(F32)
        for z in range(4):
            at = span(i, z)
            g = (residual[:, at].astype(F32) + acc[:, z * 128:(z + 1) * 128]).astype(BF16)
            gr_out[:, at] = g
            rows[i, mine, z * 128:(z + 1) * 128] = g
        for d in range(1, NT):
            ag(i, d).start()

    def ls(i):
        return rc(lgb.at[pair[i], :, :, 1 - c], lgr.at[pair[i]], ls_s.at[i], ls_r.at[i], sib)

    def stage_c(i):
        for d in range(1, NT):
            ag_in(i, d).wait_recv()
        g = rows[i]
        lg = lax.dot_general(g, teacher[...], (((0,), (0,)), ((), ())), preferred_element_type=F32)
        lg = lg.reshape(4, 2, 2, 32, 384)
        lgf[pair[i]] = lg
        lgb[pair[i]] = lg.astype(BF16)
        ls(i).start()
        w = wall[pair[i], :, :, :, :, :1024].reshape(512, 1024)
        h = jnp.dot(g, w, preferred_element_type=F32)
        if i == 0:
            hgrad[...] = h
        else:
            hgrad[...] += h

    sib_wait(0)
    for n in range(4):
        y_unit(1, n)
    sib_wait(1)
    stage_a(0)
    for s in (2, 3, 4):
        y_unit(s, 0)
        y_unit(s, 1)
        stage_b(s - 2)
        y_unit(s, 2)
        y_unit(s, 3)
        sib_wait(s)
        stage_a(s - 1)
        stage_c(s - 2)
    stage_b(3)
    stage_c(3)

    for i in range(4):
        ls(i).wait_recv()

    def own(yy, zs):
        k, p = lax.div(yy, 2), lax.rem(yy, 2)
        return lgf[k, zs:zs + 2, p, c] + lgr[k, zs:zs + 2, p].astype(F32)

    def ry(d, s, h):
        return rc(ysend.at[d, s - 1, h], yland.at[d, s - 1, h], ry_s.at[d, s - 1, h], ry_r.at[d, s - 1, h], (up_y, dn_y)[d])

    def ring(s):
        for h in (0, 1):
            for d in (0, 1):
                if s == 1 and h != d:
                    continue
                sign = 1 - 2 * d
                t = own(ymod(sign * (5 - s)), 2 * h)
                if s > 2 or (s == 2 and h == d):
                    ry(d, s - 1, h).wait_recv()
                    t = t + yland[d, s - 2, h].astype(F32)
                ysend[d, s - 1, h] = t.astype(BF16)
                ry(d, s, h).start()

    def backward(r0, r1):
        @pl.loop(r0, r1)
        def _(r):
            at = pl.ds(pl.multiple_of(r * 32, 32), 32)
            g = gate[at, :].astype(F32)
            u = up[at, :].astype(F32)
            hg = hgrad[at, :]
            sig = jax.nn.sigmoid(g)
            gu_out[at, :] = (hg * g * sig).astype(BF16)
            gg_out[at, :] = (hg * u * sig * (1.0 + g * (1.0 - sig))).astype(BF16)

    for s in (1, 2, 3, 4):
        ring(s)
        backward(2 * s - 2, 2 * s)

    for h in (0, 1):
        t = own(y, 2 * h)
        for d in (0, 1):
            ry(d, 4, h).wait_recv()
            t = t + yland[d, 3, h].astype(F32)
        zsend[2 * h:2 * h + 2] = t
    for z in range(4):
        zland[3, z] = zsend[z].astype(BF16)

    def rz(q):
        return rc(zland.at[3, zmod(q)], zland.at[q - 1, 0], bz_s.at[q - 1], bz_r.at[q - 1], zdev(q))

    for q in (1, 3, 2):
        rz(q).start()
    t = zsend[zh]
    for q in (1, 3, 2):
        rz(q).wait_recv()
        t = t + zland[q - 1, 0].astype(F32)
    pg_out[...] = t * (1.0 / 128.0)

    for q in (1, 2, 3):
        wz(q).wait_send()
        rz(q).wait_send()
    for d in (0, 1):
        for n in range(4):
            j = GRAY[n]
            for s in range(0, 5):
                if s == 0 and d == 1:
                    continue
                if s == 4 and (n >= 2) != (d == 1):
                    continue
                ws(d, s, j, c).wait_send()
                if s > 0:
                    wy(d, s, j).wait_send()
        for h in (0, 1):
            for s in range(1, 5):
                if s == 1 and h != d:
                    continue
                ry(d, s, h).wait_send()
    for i in range(4):
        ls(i).wait_send()
        for d in range(1, NT):
            ex(i, d).wait_send()
            ag(i, d).wait_send()


def per_device(teacher, projector, residual, gate_pre, up_pre, down_weight):
    vm = pl.BlockSpec(memory_space=pltpu.VMEM)
    dma = pltpu.SemaphoreType.DMA
    pg, gr, gg, gu = pl.pallas_call(
        kernel,
        out_shape=(
            jax.ShapeDtypeStruct((32, 384), F32),
            jax.ShapeDtypeStruct((32, 2048), BF16),
            jax.ShapeDtypeStruct((256, 1024), BF16),
            jax.ShapeDtypeStruct((256, 1024), BF16),
        ),
        in_specs=[vm] * 6,
        out_specs=(vm,) * 4,
        scratch_shapes=[
            pltpu.VMEM((4, 4, 2, 2, 32, 1408), BF16),
            pltpu.VMEM((256, 1408), BF16),
            pltpu.VMEM((4, 256, 512), BF16),
            pltpu.VMEM((4, 7, 32, 512), BF16),
            pltpu.VMEM((4, 256, 512), BF16),
            pltpu.VMEM((256, 1024), F32),
            pltpu.VMEM((4, 4, 2, 2, 32, 384), F32),
            pltpu.VMEM((4, 4, 2, 2, 32, 384), BF16),
            pltpu.VMEM((4, 4, 2, 32, 384), BF16),
            pltpu.VMEM((2, 4, 2, 2, 32, 384), BF16),
            pltpu.VMEM((2, 4, 2, 2, 32, 384), BF16),
            pltpu.VMEM((4, 32, 384), F32),
            pltpu.VMEM((4, 4, 32, 384), BF16),
            dma((3,)), dma((3,)), dma((3,)), dma((3,)),
            dma((2, 4, 4)), dma((2, 4, 4)), dma((2, 5, 4)), dma((2, 5, 4)),
            dma((4, 7)), dma((4, 7)), dma((4, 7)), dma((4, 7)),
            dma((4,)), dma((4,)), dma((2, 4, 2)), dma((2, 4, 2)),
        ],
        compiler_params=pltpu.CompilerParams(
            collective_id=0, has_side_effects=True, vmem_limit_bytes=56 * 1024 * 1024
        ),
        cost_estimate=pl.CostEstimate(flops=2950000000, bytes_accessed=4000000, transcendentals=524288),
    )(down_weight.T, projector.T, teacher, residual, gate_pre, up_pre)
    return pg.T, gr, gg, gu


def solution(mesh):
    in_specs = (
        P("dp", "tensor"),
        P("tensor", "dp"),
        P(("dp", "tensor"), None),
        P("dp", "tensor"),
        P("dp", "tensor"),
        P("tensor", "dp"),
    )
    out_specs = (P("tensor", "dp"), P(("dp", "tensor"), None), P("dp", "tensor"), P("dp", "tensor"))
    return jax.shard_map(
        per_device, mesh=mesh, in_specs=in_specs, out_specs=out_specs, check_vma=False
    )
```

```python
import math

import jax
import jax.numpy as jnp
from jax import lax
from jax.experimental import pallas as pl
from jax.experimental.pallas import tpu as pltpu
from jax.sharding import PartitionSpec as P

NY, NZ, NT = 8, 4, 8
MESH = pl.DeviceIdType.MESH
F32, BF16 = jnp.float32, jnp.bfloat16
CHUNKS = (
    ((0, 0),),
    ((0, 1),),
    ((1, 0), (3, 0)),
    ((0, 2), (1, 1), (3, 1)),
    ((2, 0), (0, 3)),
    ((2, 1), (1, 2), (3, 2)),
    ((1, 3), (3, 3), (2, 2)),
    ((2, 3),),
)
NC = len(CHUNKS)
WIDE = 128 * max(len(ch) for ch in CHUNKS)
YORD = (4, 3, 5, 2, 6, 1, 7)


def kernel(
    w_in, p_in, teacher_in, residual_in, gate_in, up_in,
    pg_out, gr_out, gg_out, gu_out,
    teacher, residual, gate, up,
    wall, hid, parts, rbuf, rows, hgrad, lgf, lgb, lgr, acc0, ysend, yland, zsend, zland, fsend, fland,
    in_s, wz_s, wz_r, wy_s, wy_r, ws_s, ws_r, ex_s, ex_r, ag_s, ag_r,
    ls_s, ls_r, ry_s, ry_r, rz_s, rz_r, rf_s, rf_r,
):
    dp = lax.axis_index("dp")
    me = lax.axis_index("tensor")
    c = lax.rem(dp, 2)
    y = lax.rem(lax.div(dp, 2), NY)
    zh = lax.div(dp, 2 * NY)

    def dev(cc, yy, zz, tt):
        return ((zz * NY + yy) * 2 + cc, tt)

    def ymod(s):
        return lax.rem(y + s + NY, NY)

    def zmod(s):
        return lax.rem(zh + s + NZ, NZ)

    sib = dev(1 - c, y, zh, me)
    ydev = (dev(c, ymod(1), zh, me), dev(c, ymod(-1), zh, me))

    def zdev(q):
        return dev(c, y, zmod(q), me)

    def tdev(d):
        return (dp, lax.rem(me + d, NT))

    barrier = pltpu.get_barrier_semaphore()
    peers = [sib] + [dev(c, ymod(d), zh, me) for d in range(1, NY)] + [zdev(q) for q in (1, 2, 3)] + [tdev(d) for d in range(1, NT)]
    for to in peers:
        pl.semaphore_signal(barrier, inc=1, device_id=to, device_id_type=MESH)

    loads = [
        pltpu.make_async_copy(w_in, wall.at[zh, y, c, :, 0:1024], in_s.at[0]),
        pltpu.make_async_copy(p_in, wall.at[zh, y, c, :, 1024:1408], in_s.at[1]),
        pltpu.make_async_copy(gate_in, gate, in_s.at[2]),
        pltpu.make_async_copy(up_in, up, in_s.at[3]),
        pltpu.make_async_copy(teacher_in, teacher, in_s.at[4]),
        pltpu.make_async_copy(residual_in, residual, in_s.at[5]),
    ]
    for load in loads:
        load.start()
    loads[0].wait()
    loads[1].wait()
    pl.semaphore_wait(barrier, len(peers))

    pend = {}

    def go(key, send, recv):
        send.start()
        pend[key] = [send, recv, False]

    def got(key):
        pend[key][1].wait_recv()
        pend[key][2] = True

    def drain():
        for send, recv, done in pend.values():
            if not done:
                recv.wait_recv()
        for send, recv, done in pend.values():
            send.wait_send()

    def rc(src, dst, ssem, rsem, to):
        return pltpu.make_async_remote_copy(
            src_ref=src, dst_ref=dst, send_sem=ssem, recv_sem=rsem,
            device_id=to, device_id_type=MESH,
        )

    def half(u, d):
        return u.at[16 * d:16 * d + 16, :]

    def copy_z(q):
        def at(z):
            u = wall.at[z, y, c]
            return rc(u, u, wz_s.at[q], wz_r.at[q], zdev(q))
        go(("wz", q), at(zh), at(zmod(-q)))

    def relay_z(d):
        def at(z):
            u = half(wall.at[z, y, c], d)
            return rc(u, u, wz_s.at[2 * d], wz_r.at[2 * d], zdev((1, -1)[d]))
        go(("wz2", d), at(zmod((-1, 1)[d])), at(zmod(2)))

    def copy_y(d, s, j):
        sign = 1 - 2 * d

        def at(yy):
            u = wall.at[zmod(-j), yy, c]
            if s == 4:
                u = half(u, d)
            return rc(u, u, wy_s.at[d, s - 1, j], wy_r.at[d, s - 1, j], ydev[d])
        go(("wy", d, s, j), at(ymod(-sign * (s - 1))), at(ymod(-sign * s)))

    def share(d, s, j):
        sign = 1 - 2 * d

        def at(cc):
            u = wall.at[zmod(-j), ymod(-sign * s), cc]
            if s == 4:
                u = half(u, d)
            return rc(u, u, ws_s.at[d, s, j], ws_r.at[d, s, j], sib)
        go(("ws", d, s, j), at(c), at(1 - c))

    def first(j):
        for d in (0, 1):
            copy_y(d, 1, j)
        share(0, 0, j)

    def unit(s, j):
        for d in (0, 1):
            got(("wy", d, s, j))
            if s < 4:
                copy_y(d, s + 1, j)
            share(d, s, j)

    def need(j, last):
        for s in range(last + 1):
            for d in (0, 1):
                if (s > 0 or d == 0) and not pend[("ws", d, s, j)][2]:
                    got(("ws", d, s, j))

    def make_hidden():
        for load in loads[2:5]:
            load.wait()

        @pl.loop(0, 8)
        def _(r):
            at = pl.ds(pl.multiple_of(r * 32, 32), 32)
            g = gate[at, :].astype(F32)
            u = up[at, :].astype(F32)
            hid[at, :1024] = (g * jax.nn.sigmoid(g) * u).astype(BF16)
            hid[at, 1024:] = -teacher[at, :]

    mine = pl.ds(pl.multiple_of(me * 32, 32), 32)
    k0 = lax.div(y, 2)
    turn = 2 * lax.rem(y, 2) - 1
    pair = (k0, lax.rem(k0 + turn + 4, 4), lax.rem(k0 - turn + 4, 4), lax.rem(k0 + 2, 4))

    def two(p):
        return pl.ds(2 * pair[p], 2)

    def cut(i):
        return slice(128 * i, 128 * i + 128)

    def stage_a(n):
        w = 128 * len(CHUNKS[n])
        for i, (j, p) in enumerate(CHUNKS[n]):
            need(j, p + 1)
            wt = wall[zmod(-j), two(p)].reshape(128, 1408)
            out = lax.dot_general(hid[...], wt, (((1,), (1,)), ((), ())), preferred_element_type=F32)
            parts[n, :, cut(i)] = out.astype(BF16)
        for d in YORD:
            give = pl.ds(pl.multiple_of(lax.rem(me + d, NT) * 32, 32), 32)
            copy = rc(
                parts.at[n, give, 0:w], rbuf.at[n, d - 1, :, 0:w],
                ex_s.at[n, d - 1], ex_r.at[n, d - 1], tdev(d),
            )
            go(("ex", n, d), copy, copy)

    def stage_b(n):
        w = 128 * len(CHUNKS[n])
        acc = parts[n, mine, 0:w].astype(F32)
        for d in YORD:
            got(("ex", n, d))
            acc = acc + rbuf[n, d - 1, :, 0:w].astype(F32)
        for i, (j, p) in enumerate(CHUNKS[n]):
            cols = pl.ds(pl.multiple_of(zmod(-j) * 512 + pair[p] * 128, 128), 128)
            g = (acc[:, cut(i)] + residual[:, cols].astype(F32)).astype(BF16)
            gr_out[:, cols] = g
            rows[n, mine, cut(i)] = g

        def copy(d, who):
            r = rows.at[n, pl.ds(pl.multiple_of(who * 32, 32), 32), 0:w]
            return rc(r, r, ag_s.at[n, d - 1], ag_r.at[n, d - 1], tdev(d))
        for d in YORD:
            go(("ag", n, d), copy(d, me), copy(d, lax.rem(me - d + NT, NT)))

    def stage_c(n):
        for d in YORD:
            got(("ag", n, d))
        for i, (j, p) in enumerate(CHUNKS[n]):
            lg = lax.dot_general(
                rows[n, :, cut(i)], teacher[...], (((0,), (0,)), ((), ())), preferred_element_type=F32
            ).reshape(2, 2, 32, 384)
            lgf[j, two(p)] = lg
            lgb[j, two(p)] = lg.astype(BF16)
            copy = rc(
                lgb.at[j, two(p), 1 - c], lgr.at[j, two(p)], ls_s.at[j, p], ls_r.at[j, p], sib,
            )
            go(("ls", j, p), copy, copy)

    def stage_h(n):
        h = None
        for i, (j, p) in enumerate(CHUNKS[n]):
            wt = wall[zmod(-j), two(p), :, :, :1024].reshape(128, 1024)
            one = jnp.dot(rows[n, :, cut(i)], wt, preferred_element_type=F32)
            h = one if h is None else h + one
        if n == 0:
            hgrad[...] = h
        else:
            hgrad[...] += h

    def paired(n):
        for j, p in CHUNKS[n]:
            got(("ls", j, p))
            if j == 2:
                continue
            t = lgf[j, two(p), c] + lgr[j, two(p)].astype(F32)
            if j == 0:
                acc0[two(p)] = t
            else:
                q = j // 2
                zsend[q, two(p)] = t.astype(BF16)
                copy = rc(
                    zsend.at[q, two(p)], zland.at[q, two(p)], rz_s.at[q, p], rz_r.at[q, p], zdev(-j),
                )
                go(("rz", q, p), copy, copy)

    def along_y(k):
        def copy(d):
            return rc(
                ysend.at[k, ymod(d)], yland.at[k, d - 1], ry_s.at[k, d - 1], ry_r.at[k, d - 1],
                dev(c, ymod(d), zh, me),
            )
        for d in YORD:
            go(("ry", k, d), copy(d), copy(d))

    def near_sum():
        for q in (0, 1):
            for p in range(4):
                got(("rz", q, p))
        acc0[...] += zland[0].astype(F32) + zland[1].astype(F32)
        ysend[0] = acc0[...].astype(BF16)
        along_y(0)

    def far_sum():
        ysend[1] = (lgf[2, :, c] + lgr[2].astype(F32)).astype(BF16)
        along_y(1)

    def far_end():
        t = lgf[2, y, c] + lgr[2, y].astype(F32)
        for d in YORD[::-1]:
            got(("ry", 1, d))
            t = t + yland[1, d - 1].astype(F32)
        fsend[...] = t.astype(BF16)
        copy = rc(fsend, fland, rf_s, rf_r, zdev(2))
        go(("rf",), copy, copy)

    def near_end():
        t = acc0[y]
        for d in YORD[::-1]:
            got(("ry", 0, d))
            t = t + yland[0, d - 1].astype(F32)
        pg_out[...] = t

    def end():
        got(("rf",))
        pg_out[...] = (pg_out[...] + fland[...].astype(F32)) * (1.0 / math.sqrt(256 * 64))
        drain()

    def backward(r0, r1):
        @pl.loop(r0, r1)
        def _(r):
            at = pl.ds(pl.multiple_of(r * 32, 32), 32)
            g = gate[at, :].astype(F32)
            u = up[at, :].astype(F32)
            hg = hgrad[at, :]
            sig = jax.nn.sigmoid(g)
            gu_out[at, :] = (hg * g * sig).astype(BF16)
            gg_out[at, :] = (hg * u * sig * (1.0 + g * (1.0 - sig))).astype(BF16)

    copy_z(1)
    copy_z(3)
    first(0)
    make_hidden()
    unit(1, 0)
    got(("wz", 1))
    first(1)
    relay_z(0)
    got(("wz", 3))
    relay_z(1)
    first(3)
    stage_a(0)
    unit(2, 0)
    unit(1, 1)
    stage_a(1)
    loads[5].wait()
    unit(1, 3)
    stage_b(0)
    unit(3, 0)
    got(("wz2", 0))
    got(("wz2", 1))
    first(2)
    stage_a(2)
    unit(2, 1)
    stage_b(1)
    unit(2, 3)
    unit(4, 0)
    unit(1, 2)
    stage_a(3)
    stage_b(2)
    unit(3, 1)
    stage_c(0)
    stage_h(0)
    unit(3, 3)
    stage_a(4)
    unit(2, 2)
    stage_c(1)
    stage_h(1)
    unit(4, 1)
    stage_b(3)
    stage_a(5)
    unit(4, 3)
    unit(3, 2)
    stage_b(4)
    stage_c(2)
    stage_h(2)
    stage_a(6)
    paired(0)
    paired(1)
    unit(4, 2)
    stage_c(3)
    stage_h(3)
    stage_b(5)
    stage_a(7)
    paired(2)
    stage_c(4)
    stage_h(4)
    stage_b(6)
    paired(3)
    stage_c(5)
    stage_h(5)
    stage_b(7)
    paired(4)
    stage_c(6)
    paired(5)
    stage_c(7)
    paired(6)
    paired(7)
    far_sum()
    stage_h(6)
    stage_h(7)
    near_sum()
    backward(0, 8)
    far_end()
    near_end()
    end()


def finish(a, b, c, d, oa, ob, oc, od):
    for x, o in ((a, oa), (b, ob), (c, oc), (d, od)):
        o[...] = x[...]


def per_device(teacher, projector, residual, gate_pre, up_pre, down_weight):
    vm = pl.BlockSpec(memory_space=pltpu.VMEM)
    hbm = pl.BlockSpec(memory_space=pl.ANY)
    dma = pltpu.SemaphoreType.DMA
    outs = (
        jax.ShapeDtypeStruct((32, 384), F32),
        jax.ShapeDtypeStruct((32, 2048), BF16),
        jax.ShapeDtypeStruct((256, 1024), BF16),
        jax.ShapeDtypeStruct((256, 1024), BF16),
    )
    results = pl.pallas_call(
        kernel,
        out_shape=outs,
        in_specs=[hbm] * 6,
        out_specs=(vm,) * 4,
        scratch_shapes=[
            pltpu.VMEM((256, 384), BF16),
            pltpu.VMEM((32, 2048), BF16),
            pltpu.VMEM((256, 1024), BF16),
            pltpu.VMEM((256, 1024), BF16),
            pltpu.VMEM((4, 8, 2, 32, 1408), BF16),
            pltpu.VMEM((256, 1408), BF16),
            pltpu.VMEM((NC, 256, WIDE), BF16),
            pltpu.VMEM((NC, 7, 32, WIDE), BF16),
            pltpu.VMEM((NC, 256, WIDE), BF16),
            pltpu.VMEM((256, 1024), F32),
            pltpu.VMEM((4, 8, 2, 32, 384), F32),
            pltpu.VMEM((4, 8, 2, 32, 384), BF16),
            pltpu.VMEM((4, 8, 32, 384), BF16),
            pltpu.VMEM((8, 32, 384), F32),
            pltpu.VMEM((2, 8, 32, 384), BF16),
            pltpu.VMEM((2, 7, 32, 384), BF16),
            pltpu.VMEM((2, 8, 32, 384), BF16),
            pltpu.VMEM((2, 8, 32, 384), BF16),
            pltpu.VMEM((32, 384), BF16),
            pltpu.VMEM((32, 384), BF16),
            dma((6,)), dma((4,)), dma((4,)),
            dma((2, 4, 4)), dma((2, 4, 4)), dma((2, 5, 4)), dma((2, 5, 4)),
            dma((NC, 7)), dma((NC, 7)), dma((NC, 7)), dma((NC, 7)),
            dma((4, 4)), dma((4, 4)), dma((2, 7)), dma((2, 7)), dma((2, 4)), dma((2, 4)), dma(()), dma(()),
        ],
        compiler_params=pltpu.CompilerParams(
            collective_id=0, has_side_effects=True, vmem_limit_bytes=56 * 1024 * 1024
        ),
        cost_estimate=pl.CostEstimate(flops=2950000000, bytes_accessed=4000000, transcendentals=524288),
    )(down_weight.T, projector.T, teacher, residual, gate_pre, up_pre)
    pg, gr, gg, gu = pl.pallas_call(
        finish,
        out_shape=outs,
        in_specs=[vm] * 4,
        out_specs=(vm,) * 4,
    )(*results)
    return pg.T, gr, gg, gu


def solution(mesh):
    in_specs = (
        P("dp", "tensor"),
        P("tensor", "dp"),
        P(("dp", "tensor"), None),
        P("dp", "tensor"),
        P("dp", "tensor"),
        P("tensor", "dp"),
    )
    out_specs = (P("tensor", "dp"), P(("dp", "tensor"), None), P("dp", "tensor"), P("dp", "tensor"))
    return jax.shard_map(
        per_device, mesh=mesh, in_specs=in_specs, out_specs=out_specs, check_vma=False
    )
```

```python
import math

import jax
import jax.numpy as jnp
from jax import lax
from jax.experimental import pallas as pl
from jax.experimental.pallas import tpu as pltpu
from jax.sharding import PartitionSpec as P

NY, NZ, NT = 8, 4, 8
MESH = pl.DeviceIdType.MESH
F32, BF16 = jnp.float32, jnp.bfloat16
CHUNKS = (
    ((0, 0),),
    ((0, 1),),
    ((1, 0), (3, 0)),
    ((0, 2), (1, 1), (3, 1)),
    ((2, 0), (0, 3)),
    ((2, 1), (1, 2), (3, 2)),
    ((1, 3), (3, 3), (2, 2)),
    ((2, 3),),
)
NC = len(CHUNKS)
WIDE = 128 * max(len(ch) for ch in CHUNKS)
YORD = (4, 3, 5, 2, 6, 1, 7)


def kernel(
    w_in, p_in, teacher_in, residual_in, gate_in, up_in,
    pg_out, gr_out, gg_out, gu_out,
    teacher, residual, gate, up,
    wall, hid, parts, rbuf, rows, hgrad, lgf, lgb, lgr, acc0, ysend, yland, zsend, zland, fsend, fland,
    in_s, wz_s, wz_r, wy_s, wy_r, ws_s, ws_r, ex_s, ex_r, ag_s, ag_r,
    ls_s, ls_r, ry_s, ry_r, rz_s, rz_r, rf_s, rf_r,
):
    dp = lax.axis_index("dp")
    me = lax.axis_index("tensor")
    c = lax.rem(dp, 2)
    y = lax.rem(lax.div(dp, 2), NY)
    zh = lax.div(dp, 2 * NY)

    def dev(cc, yy, zz, tt):
        return ((zz * NY + yy) * 2 + cc, tt)

    def ymod(s):
        return lax.rem(y + s + NY, NY)

    def zmod(s):
        return lax.rem(zh + s + NZ, NZ)

    sib = dev(1 - c, y, zh, me)
    ydev = (dev(c, ymod(1), zh, me), dev(c, ymod(-1), zh, me))

    def zdev(q):
        return dev(c, y, zmod(q), me)

    def tdev(d):
        return (dp, lax.rem(me + d, NT))

    barrier = pltpu.get_barrier_semaphore()
    peers = [sib] + [dev(c, ymod(d), zh, me) for d in range(1, NY)] + [zdev(q) for q in (1, 2, 3)] + [tdev(d) for d in range(1, NT)]
    for to in peers:
        pl.semaphore_signal(barrier, inc=1, device_id=to, device_id_type=MESH)

    loads = [
        pltpu.make_async_copy(w_in, wall.at[zh, y, c, :, 0:1024], in_s.at[0]),
        pltpu.make_async_copy(p_in, wall.at[zh, y, c, :, 1024:1408], in_s.at[1]),
        pltpu.make_async_copy(gate_in, gate, in_s.at[2]),
        pltpu.make_async_copy(up_in, up, in_s.at[3]),
        pltpu.make_async_copy(teacher_in, teacher, in_s.at[4]),
        pltpu.make_async_copy(residual_in, residual, in_s.at[5]),
    ]
    for load in loads:
        load.start()
    loads[0].wait()
    loads[1].wait()
    pl.semaphore_wait(barrier, len(peers))

    pend = {}

    def go(key, send, recv):
        send.start()
        pend[key] = [send, recv, False]

    def got(key):
        pend[key][1].wait_recv()
        pend[key][2] = True

    def drain():
        for send, recv, done in pend.values():
            if not done:
                recv.wait_recv()
        for send, recv, done in pend.values():
            send.wait_send()

    def rc(src, dst, ssem, rsem, to):
        return pltpu.make_async_remote_copy(
            src_ref=src, dst_ref=dst, send_sem=ssem, recv_sem=rsem,
            device_id=to, device_id_type=MESH,
        )

    def half(u, d):
        return u.at[16 * d:16 * d + 16, :]

    def copy_z(q):
        def at(z):
            u = wall.at[z, y, c]
            return rc(u, u, wz_s.at[q], wz_r.at[q], zdev(q))
        go(("wz", q), at(zh), at(zmod(-q)))

    def relay_z(d):
        def at(z):
            u = half(wall.at[z, y, c], d)
            return rc(u, u, wz_s.at[2 * d], wz_r.at[2 * d], zdev((1, -1)[d]))
        go(("wz2", d), at(zmod((-1, 1)[d])), at(zmod(2)))

    def copy_y(d, s, j):
        sign = 1 - 2 * d

        def at(yy):
            u = wall.at[zmod(-j), yy, c]
            if s == 4:
                u = half(u, d)
            return rc(u, u, wy_s.at[d, s - 1, j], wy_r.at[d, s - 1, j], ydev[d])
        go(("wy", d, s, j), at(ymod(-sign * (s - 1))), at(ymod(-sign * s)))

    def share(d, s, j):
        sign = 1 - 2 * d

        def at(cc):
            u = wall.at[zmod(-j), ymod(-sign * s), cc]
            if s == 4:
                u = half(u, d)
            return rc(u, u, ws_s.at[d, s, j], ws_r.at[d, s, j], sib)
        go(("ws", d, s, j), at(c), at(1 - c))

    def first(j):
        for d in (0, 1):
            copy_y(d, 1, j)
        share(0, 0, j)

    def unit(s, j):
        for d in (0, 1):
            got(("wy", d, s, j))
            if s < 4:
                copy_y(d, s + 1, j)
            share(d, s, j)

    def need(j, last):
        for s in range(last + 1):
            for d in (0, 1):
                if (s > 0 or d == 0) and not pend[("ws", d, s, j)][2]:
                    got(("ws", d, s, j))

    def make_hidden():
        for load in loads[2:5]:
            load.wait()

        @pl.loop(0, 8)
        def _(r):
            at = pl.ds(pl.multiple_of(r * 32, 32), 32)
            g = gate[at, :].astype(F32)
            u = up[at, :].astype(F32)
            hid[at, :1024] = (g * jax.nn.sigmoid(g) * u).astype(BF16)
            hid[at, 1024:] = -teacher[at, :]

    mine = pl.ds(pl.multiple_of(me * 32, 32), 32)
    k0 = lax.div(y, 2)
    turn = 2 * lax.rem(y, 2) - 1
    pair = (k0, lax.rem(k0 + turn + 4, 4), lax.rem(k0 - turn + 4, 4), lax.rem(k0 + 2, 4))

    def two(p):
        return pl.ds(2 * pair[p], 2)

    def cut(i):
        return slice(128 * i, 128 * i + 128)

    def stage_a(n):
        w = 128 * len(CHUNKS[n])
        for i, (j, p) in enumerate(CHUNKS[n]):
            need(j, p + 1)
            wt = wall[zmod(-j), two(p)].reshape(128, 1408)
            out = lax.dot_general(hid[...], wt, (((1,), (1,)), ((), ())), preferred_element_type=F32)
            parts[n, :, cut(i)] = out.astype(BF16)
        for d in YORD:
            give = pl.ds(pl.multiple_of(lax.rem(me + d, NT) * 32, 32), 32)
            copy = rc(
                parts.at[n, give, 0:w], rbuf.at[n, d - 1, :, 0:w],
                ex_s.at[n, d - 1], ex_r.at[n, d - 1], tdev(d),
            )
            go(("ex", n, d), copy, copy)

    def stage_b(n):
        w = 128 * len(CHUNKS[n])
        acc = parts[n, mine, 0:w].astype(F32)
        for d in YORD:
            got(("ex", n, d))
            acc = acc + rbuf[n, d - 1, :, 0:w].astype(F32)
        for i, (j, p) in enumerate(CHUNKS[n]):
            cols = pl.ds(pl.multiple_of(zmod(-j) * 512 + pair[p] * 128, 128), 128)
            g = (acc[:, cut(i)] + residual[:, cols].astype(F32)).astype(BF16)
            gr_out[:, cols] = g
            rows[n, mine, cut(i)] = g

        def copy(d, who):
            r = rows.at[n, pl.ds(pl.multiple_of(who * 32, 32), 32), 0:w]
            return rc(r, r, ag_s.at[n, d - 1], ag_r.at[n, d - 1], tdev(d))
        for d in YORD:
            go(("ag", n, d), copy(d, me), copy(d, lax.rem(me - d + NT, NT)))

    def stage_c(n):
        for d in YORD:
            got(("ag", n, d))
        for i, (j, p) in enumerate(CHUNKS[n]):
            lg = lax.dot_general(
                rows[n, :, cut(i)], teacher[...], (((0,), (0,)), ((), ())), preferred_element_type=F32
            ).reshape(2, 2, 32, 384)
            lgf[j, two(p)] = lg
            lgb[j, two(p)] = lg.astype(BF16)
            copy = rc(
                lgb.at[j, two(p), 1 - c], lgr.at[j, two(p)], ls_s.at[j, p], ls_r.at[j, p], sib,
            )
            go(("ls", j, p), copy, copy)

    def stage_h(n):
        h = None
        for i, (j, p) in enumerate(CHUNKS[n]):
            wt = wall[zmod(-j), two(p), :, :, :1024].reshape(128, 1024)
            one = jnp.dot(rows[n, :, cut(i)], wt, preferred_element_type=F32)
            h = one if h is None else h + one
        if n == 0:
            hgrad[...] = h
        else:
            hgrad[...] += h

    def paired(n):
        for j, p in CHUNKS[n]:
            got(("ls", j, p))
            if j == 2:
                continue
            t = lgf[j, two(p), c] + lgr[j, two(p)].astype(F32)
            if j == 0:
                acc0[two(p)] = t
            else:
                q = j // 2
                zsend[q, two(p)] = t.astype(BF16)
                copy = rc(
                    zsend.at[q, two(p)], zland.at[q, two(p)], rz_s.at[q, p], rz_r.at[q, p], zdev(-j),
                )
                go(("rz", q, p), copy, copy)

    def along_y(k):
        def copy(d):
            return rc(
                ysend.at[k, ymod(d)], yland.at[k, d - 1], ry_s.at[k, d - 1], ry_r.at[k, d - 1],
                dev(c, ymod(d), zh, me),
            )
        for d in YORD:
            go(("ry", k, d), copy(d), copy(d))

    def near_sum():
        for q in (0, 1):
            for p in range(4):
                got(("rz", q, p))
        acc0[...] += zland[0].astype(F32) + zland[1].astype(F32)
        ysend[0] = acc0[...].astype(BF16)
        along_y(0)

    def far_sum():
        ysend[1] = (lgf[2, :, c] + lgr[2].astype(F32)).astype(BF16)
        along_y(1)

    def far_end():
        t = lgf[2, y, c] + lgr[2, y].astype(F32)
        for d in YORD[::-1]:
            got(("ry", 1, d))
            t = t + yland[1, d - 1].astype(F32)
        fsend[...] = t.astype(BF16)
        copy = rc(fsend, fland, rf_s, rf_r, zdev(2))
        go(("rf",), copy, copy)

    def near_end():
        t = acc0[y]
        for d in YORD[::-1]:
            got(("ry", 0, d))
            t = t + yland[0, d - 1].astype(F32)
        pg_out[...] = t

    def end():
        got(("rf",))
        pg_out[...] = (pg_out[...] + fland[...].astype(F32)) * (1.0 / math.sqrt(256 * 64))
        drain()

    def backward(r0, r1):
        @pl.loop(r0, r1)
        def _(r):
            at = pl.ds(pl.multiple_of(r * 32, 32), 32)
            g = gate[at, :].astype(F32)
            u = up[at, :].astype(F32)
            hg = hgrad[at, :]
            sig = jax.nn.sigmoid(g)
            gu_out[at, :] = (hg * g * sig).astype(BF16)
            gg_out[at, :] = (hg * u * sig * (1.0 + g * (1.0 - sig))).astype(BF16)

    copy_z(1)
    copy_z(3)
    first(0)
    make_hidden()
    unit(1, 0)
    got(("wz", 1))
    first(1)
    relay_z(0)
    got(("wz", 3))
    relay_z(1)
    first(3)
    stage_a(0)
    unit(2, 0)
    unit(1, 1)
    stage_a(1)
    loads[5].wait()
    unit(1, 3)
    stage_b(0)
    unit(3, 0)
    got(("wz2", 0))
    got(("wz2", 1))
    first(2)
    stage_a(2)
    unit(2, 1)
    stage_b(1)
    unit(2, 3)
    unit(4, 0)
    unit(1, 2)
    stage_a(3)
    stage_b(2)
    unit(3, 1)
    stage_c(0)
    stage_h(0)
    unit(3, 3)
    stage_a(4)
    unit(2, 2)
    stage_c(1)
    stage_h(1)
    unit(4, 1)
    stage_b(3)
    stage_a(5)
    unit(4, 3)
    unit(3, 2)
    stage_b(4)
    stage_c(2)
    stage_h(2)
    stage_a(6)
    paired(0)
    paired(1)
    unit(4, 2)
    stage_c(3)
    stage_h(3)
    stage_b(5)
    stage_a(7)
    paired(2)
    stage_c(4)
    stage_b(6)
    paired(3)
    stage_b(7)
    stage_h(4)
    stage_c(5)
    paired(4)
    stage_h(5)
    stage_c(6)
    paired(5)
    paired(6)
    stage_c(7)
    paired(7)
    far_sum()
    stage_h(6)
    stage_h(7)
    near_sum()
    backward(0, 8)
    far_end()
    near_end()
    end()


def finish(a, b, c, d, oa, ob, oc, od):
    for x, o in ((a, oa), (b, ob), (c, oc), (d, od)):
        o[...] = x[...]


def per_device(teacher, projector, residual, gate_pre, up_pre, down_weight):
    vm = pl.BlockSpec(memory_space=pltpu.VMEM)
    hbm = pl.BlockSpec(memory_space=pl.ANY)
    dma = pltpu.SemaphoreType.DMA
    outs = (
        jax.ShapeDtypeStruct((32, 384), F32),
        jax.ShapeDtypeStruct((32, 2048), BF16),
        jax.ShapeDtypeStruct((256, 1024), BF16),
        jax.ShapeDtypeStruct((256, 1024), BF16),
    )
    results = pl.pallas_call(
        kernel,
        out_shape=outs,
        in_specs=[hbm] * 6,
        out_specs=(vm,) * 4,
        scratch_shapes=[
            pltpu.VMEM((256, 384), BF16),
            pltpu.VMEM((32, 2048), BF16),
            pltpu.VMEM((256, 1024), BF16),
            pltpu.VMEM((256, 1024), BF16),
            pltpu.VMEM((4, 8, 2, 32, 1408), BF16),
            pltpu.VMEM((256, 1408), BF16),
            pltpu.VMEM((NC, 256, WIDE), BF16),
            pltpu.VMEM((NC, 7, 32, WIDE), BF16),
            pltpu.VMEM((NC, 256, WIDE), BF16),
            pltpu.VMEM((256, 1024), F32),
            pltpu.VMEM((4, 8, 2, 32, 384), F32),
            pltpu.VMEM((4, 8, 2, 32, 384), BF16),
            pltpu.VMEM((4, 8, 32, 384), BF16),
            pltpu.VMEM((8, 32, 384), F32),
            pltpu.VMEM((2, 8, 32, 384), BF16),
            pltpu.VMEM((2, 7, 32, 384), BF16),
            pltpu.VMEM((2, 8, 32, 384), BF16),
            pltpu.VMEM((2, 8, 32, 384), BF16),
            pltpu.VMEM((32, 384), BF16),
            pltpu.VMEM((32, 384), BF16),
            dma((6,)), dma((4,)), dma((4,)),
            dma((2, 4, 4)), dma((2, 4, 4)), dma((2, 5, 4)), dma((2, 5, 4)),
            dma((NC, 7)), dma((NC, 7)), dma((NC, 7)), dma((NC, 7)),
            dma((4, 4)), dma((4, 4)), dma((2, 7)), dma((2, 7)), dma((2, 4)), dma((2, 4)), dma(()), dma(()),
        ],
        compiler_params=pltpu.CompilerParams(
            collective_id=0, has_side_effects=True, vmem_limit_bytes=56 * 1024 * 1024
        ),
        cost_estimate=pl.CostEstimate(flops=2950000000, bytes_accessed=4000000, transcendentals=524288),
    )(down_weight.T, projector.T, teacher, residual, gate_pre, up_pre)
    pg, gr, gg, gu = pl.pallas_call(
        finish,
        out_shape=outs,
        in_specs=[vm] * 4,
        out_specs=(vm,) * 4,
    )(*results)
    return pg.T, gr, gg, gu


def solution(mesh):
    in_specs = (
        P("dp", "tensor"),
        P("tensor", "dp"),
        P(("dp", "tensor"), None),
        P("dp", "tensor"),
        P("dp", "tensor"),
        P("tensor", "dp"),
    )
    out_specs = (P("tensor", "dp"), P(("dp", "tensor"), None), P("dp", "tensor"), P("dp", "tensor"))
    return jax.shard_map(
        per_device, mesh=mesh, in_specs=in_specs, out_specs=out_specs, check_vma=False
    )
```
